512 devices in a mesh: rows: 16 (over x, z_hi, core), cols: 32 (over z_lo, y).
Axes of the slice: x: 4, y: 4, z: 16 (z_hi: 2, z_lo: 8; z = z_hi * 8 + z_lo), core: 2. Of those that a mesh axis runs over, the one named last changes fastest.
Arguments:
- train_hidden: bfloat16 [512, 8, 4096], P(('rows', 'cols')), may hold values from -6 to 6
- train_cotangent: bfloat16 [512, 8, 4096], P(('rows', 'cols')), may hold values from -6 to 6
- train_lengths: int32 [512], P(('rows', 'cols')), may hold values from 1 to 8, 3072 in all
- roll_hidden: bfloat16 [512, 8, 4096], P(('cols', 'rows')), may hold values from -6 to 6
- roll_cotangent: bfloat16 [512, 8, 4096], P(('cols', 'rows')), may hold values from -6 to 6
- roll_lengths: int32 [512], P(('cols', 'rows')), may hold values from 1 to 8, 3072 in all
- gate_weight: bfloat16 [4096, 14336], P('rows', 'cols'), may hold values from -0.09375 to 0.09375
- up_weight: bfloat16 [4096, 14336], P('rows', 'cols'), may hold values from -0.09375 to 0.09375
- in_project: bfloat16 [14336, 64], P('cols'), may hold values from -0.046875 to 0.046875
- out_project: bfloat16 [4096, 64], replicated, may hold values from -0.09375 to 0.09375
Outputs:
- scores: float32 [512, 512], P('rows', 'cols')
The draws below stay inside these ranges and needn't reach their ends.
All inputs are finite; a program needn't handle non-finite values. No bound on the sum of `train_lengths` or of `roll_lengths` on one device may be relied on, other than what follows from the above.
Results may differ from the reference program's by a relative error of at most 0.0041.
Values may be sent and summed in bfloat16 or wider, within the bound.
No kernel may reach another device: no remote copies, remote signals or barrier semaphores. Data moves between devices by JAX's collectives and lax.ppermute only.
A program may use at most 64 MiB of HBM per device.

```python
import math
import jax
import jax.numpy as jnp
import numpy as np
from jax import lax

D = 4096
FF = 14336
RANK = 64
L = 8
NTR = 512
NRO = 512


def levels(stream_key, dims, split, least, top_value):
    gain = 1.0
    for axis_at, blocks in split:
        draws = jax.random.uniform(jax.random.fold_in(jax.random.fold_in(stream_key, 6), axis_at), (blocks,), jnp.float32, least / len(split), top_value / len(split))
        gain = gain * jnp.repeat(jnp.exp(draws), dims[axis_at] // blocks).reshape((-1,) + (1,) * (len(dims) - 1 - axis_at))
    return gain


def split_up(count, total, limit, lean):
    portions = [(1 << 20) // math.isqrt(standing ** lean) + 1 for standing in range(2, count + 1)]
    spare, given = total - limit - (count - 1), [1] * (count - 1)
    while spare > 0:
        free = [i for i in range(count - 1) if given[i] < limit]
        pool, budget = sum([portions[i] for i in free]), spare
        for i in free:
            more = min(limit - given[i], max(1, budget * portions[i] // pool), spare)
            given[i] = given[i] + more
            spare = spare - more
    return np.array([limit] + given)


def ragged_sizes(rng, number_of, total, bound, lean):
    if number_of == 2:
        one = jax.random.randint(rng, (), max(1, total - bound), min(bound, total - 1) + 1)
        return jnp.stack([one, total - one])
    sizes = jnp.asarray(split_up(number_of, total, bound, lean), jnp.int32)
    twos = (number_of - 1) // 2
    source_of, sink = sizes[1:1 + 2 * twos:2], sizes[2:2 + 2 * twos:2]
    room = jnp.minimum(source_of - 1, bound - sink)
    shifted = jax.random.randint(jax.random.fold_in(rng, 1), (twos,), 0, 1 << 20) % (room + 1)
    sizes = sizes.at[1:1 + 2 * twos:2].set(source_of - shifted).at[2:2 + 2 * twos:2].set(sink + shifted)
    return sizes[jax.random.permutation(jax.random.fold_in(rng, 2), number_of)]


def bell_draw(key, dims, deviation, reach, pieces=(), kind=jnp.bfloat16):
    result = deviation * jax.random.normal(key, dims, jnp.float32)
    if pieces:
        result = result * levels(key, dims, pieces, -0.22, 0.18)
    return jnp.clip(result, -reach, reach).astype(kind)


def setup_inputs(seed: int = 0) -> dict:
    seeds = jax.random.split(jax.random.key(seed), 11)
    return {
        "train_hidden": bell_draw(seeds[0], (NTR, L, D), 1.0, 6.0, ((0, 512),)),
        "train_cotangent": bell_draw(seeds[1], (NTR, L, D), 1.0, 6.0, ((0, 512),)),
        "train_lengths": ragged_sizes(seeds[2], NTR, NTR * L * 3 // 4, L, 0).astype(jnp.int32),
        "roll_hidden": bell_draw(seeds[3], (NRO, L, D), 1.0, 6.0, ((0, 512),)),
        "roll_cotangent": bell_draw(seeds[4], (NRO, L, D), 1.0, 6.0, ((0, 512),)),
        "roll_lengths": ragged_sizes(seeds[5], NRO, NRO * L * 3 // 4, L, 0).astype(jnp.int32),
        "gate_weight": bell_draw(seeds[6], (D, FF), D ** -0.5, 0.09375, ((0, 16), (1, 32))),
        "up_weight": bell_draw(seeds[7], (D, FF), D ** -0.5, 0.09375, ((0, 16), (1, 32))),
        "in_project": bell_draw(seeds[8], (FF, RANK), FF ** -0.5, 0.046875, ((0, 32),)),
        "out_project": bell_draw(seeds[9], (D, RANK), D ** -0.5, 0.09375),
    }


def block_units(hidden, cotangent, lengths, gate_weight, up_weight, in_project, out_project):
    count = hidden.shape[0]
    tokens = hidden.reshape(-1, D)
    gate = jnp.dot(tokens, gate_weight, preferred_element_type=jnp.float32)
    up = jnp.dot(tokens, up_weight, preferred_element_type=jnp.float32)
    act = (jax.nn.silu(gate) * up).astype(jnp.bfloat16)
    left = jnp.dot(act, in_project, preferred_element_type=jnp.float32).reshape(count, L, RANK)
    right = jnp.dot(cotangent.reshape(-1, D), out_project, preferred_element_type=jnp.float32).reshape(count, L, RANK)
    live = (jnp.arange(L, dtype=jnp.int32)[None, :] < lengths[:, None]).astype(jnp.float32)
    grad = jnp.einsum('eta,etb->eab', left * live[:, :, None], right, precision=lax.Precision.HIGHEST).reshape(count, RANK * RANK)
    return grad / jnp.sqrt(lax.optimization_barrier(jnp.mean(grad * grad, axis=1, keepdims=True)) + 1e-06)

def all_units(hidden, cotangent, lengths, gate_weight, up_weight, in_project, out_project):
    blocks = hidden.shape[0] // 32

    def one(item):
        return block_units(item[0], item[1], item[2], gate_weight, up_weight, in_project, out_project)
    units = lax.map(one, (hidden.reshape(blocks, 32, L, D), cotangent.reshape(blocks, 32, L, D), lengths.reshape(blocks, 32)))
    return units.reshape(-1, RANK * RANK)

def reference(train_hidden, train_cotangent, train_lengths, roll_hidden, roll_cotangent, roll_lengths, gate_weight, up_weight, in_project, out_project):
    train_units = all_units(train_hidden, train_cotangent, train_lengths, gate_weight, up_weight, in_project, out_project)
    roll_units = all_units(roll_hidden, roll_cotangent, roll_lengths, gate_weight, up_weight, in_project, out_project)
    return jnp.dot(train_units, roll_units.T, precision=lax.Precision.HIGHEST) / RANK
```

```python
import functools

import jax
import jax.numpy as jnp
from jax import lax
from jax.experimental import pallas as pl
from jax.experimental.pallas import tpu as pltpu
from jax.sharding import Mesh, PartitionSpec as P

RANK = 64
NX, NZH, NCO, NZL, NY = 4, 2, 2, 8, 4
HIGH = lax.Precision.HIGHEST


def mlp_kernel(nw, xplan, wk_ref, xr_ref, *refs):
    w_refs = refs[:nw]
    x_refs = refs[nw : nw + len(xplan)]
    ip_ref, out_ref, wv, xv, acc, wsem, xsem = refs[nw + len(xplan) :]
    wcopies = [pltpu.make_async_copy(w_refs[p], wv.at[p], wsem.at[p]) for p in range(nw)]
    xcopies = []
    for i, parts in enumerate(xplan):
        for j, slot in enumerate(parts):
            row = pl.multiple_of(xr_ref[slot] * 16, 16)
            xcopies.append(
                pltpu.make_async_copy(
                    x_refs[i].at[pl.ds(16 * j, 16)], xv.at[pl.ds(row, 16)], xsem.at[slot]
                )
            )
    for c in xcopies:
        c.start()
    for c in wcopies:
        c.start()
    for c in xcopies:
        c.wait()
    for p in range(nw):
        wcopies[p].wait()
        col = pl.multiple_of(wk_ref[p] * 256, 256)
        part = jnp.dot(xv[:, pl.ds(col, 256)], wv[p], preferred_element_type=jnp.float32)
        if p == 0:
            acc[...] = part
        else:
            acc[...] += part
    half = acc.shape[1] // 2
    for m in range(4):
        rows = acc[m * 128 : (m + 1) * 128, :]
        gate, up = rows[:, :half], rows[:, half:]
        act = (gate / (1.0 + jnp.exp(-gate)) * up).astype(jnp.bfloat16)
        left = jnp.dot(act, ip_ref[...], preferred_element_type=jnp.float32)
        left = left.reshape(8, 2, 8, RANK)
        out_ref[m * 8 : (m + 1) * 8] = jnp.concatenate([left[:, 0], left[:, 1]], axis=-1)


def mlp(wk, xr, ws, xs, xplan, ip):
    nw = len(ws)
    any_ = pl.BlockSpec(memory_space=pl.ANY)
    smem = pl.BlockSpec(memory_space=pltpu.SMEM)
    return pl.pallas_call(
        functools.partial(mlp_kernel, nw, xplan),
        out_shape=jax.ShapeDtypeStruct((32, 8, 2 * RANK), jnp.float32),
        in_specs=[smem, smem] + [any_] * (nw + len(xs)) + [pl.BlockSpec(memory_space=pltpu.VMEM)],
        out_specs=pl.BlockSpec(memory_space=pltpu.VMEM),
        scratch_shapes=[
            pltpu.VMEM((nw,) + ws[0].shape, jnp.bfloat16),
            pltpu.VMEM((512, xs[0].shape[1]), jnp.bfloat16),
            pltpu.VMEM((512, ws[0].shape[1]), jnp.float32),
            pltpu.SemaphoreType.DMA((nw,)),
            pltpu.SemaphoreType.DMA((32,)),
        ],
        compiler_params=pltpu.CompilerParams(vmem_limit_bytes=40 << 20),
        name="mlp",
    )(wk, xr, *ws, *xs, ip)


def norm_kernel(parts_ref, right_ref, live_ref, train_ref, roll_ref):
    left = jnp.sum(parts_ref[...], axis=0)
    for s, ref in ((0, train_ref), (1, roll_ref)):
        one = left[:, s * RANK : (s + 1) * RANK] * live_ref[s]
        right = right_ref[s]
        grad = lax.dot_general(
            one, right, (((0,), (0,)), ((), ())), precision=HIGH, preferred_element_type=jnp.float32
        )
        mean = jnp.sum(grad * grad) / (RANK * RANK)
        inv = 1.0 / jnp.sqrt(jnp.full((8, RANK), mean + 1e-6))
        ref[...] = jnp.concatenate([one * inv, right], axis=-1)


def score_kernel(train_ref, roll_ref, out_ref):
    t = train_ref[...].reshape(-1, 2 * RANK)
    r = roll_ref[...].reshape(-1, 2 * RANK)
    dims = (((1,), (1,)), ((), ()))
    a = lax.dot_general(
        t[:, :RANK], r[:, :RANK], dims, precision=HIGH, preferred_element_type=jnp.float32
    )
    b = lax.dot_general(
        t[:, RANK:], r[:, RANK:], dims, precision=HIGH, preferred_element_type=jnp.float32
    )
    both = jnp.sum((a * b).reshape(32, 8, 128), axis=1)
    pick = (
        lax.broadcasted_iota(jnp.int32, (128, 16), 0) // 8
        == lax.broadcasted_iota(jnp.int32, (128, 16), 1)
    ).astype(jnp.float32)
    out_ref[...] = jnp.dot(both, pick, precision=HIGH, preferred_element_type=jnp.float32) / RANK


def shift(n, k):
    return [(i, (i + k) % n) for i in range(n)]


def on_device(
    train_hidden,
    train_cotangent,
    train_lengths,
    roll_hidden,
    roll_cotangent,
    roll_lengths,
    gate_weight,
    up_weight,
    in_project,
    out_project,
):
    x, zh, co, zl, y = (lax.axis_index(a) for a in ("x", "zh", "co", "zl", "y"))
    width = train_hidden.shape[2]
    own = jnp.concatenate([train_hidden[0], roll_hidden[0]], axis=0)
    w = jnp.concatenate([gate_weight, up_weight], axis=1)

    far = lax.ppermute(own, "zl", [(i, i ^ 4) for i in range(8)])
    other = lax.ppermute(w, "zh", shift(2, 1))

    xs, xplan, xr = [], [], []

    def add_x(array, spots):
        xs.append(array)
        slots = []
        for s in spots:
            slots.append(len(xr))
            xr.append(s)
        xplan.append(tuple(slots))

    def over_y(array, zls):
        add_x(array, [z * 4 + y for z in zls])
        for k in (1, 3, 2):
            add_x(lax.ppermute(array, "y", shift(NY, k)), [z * 4 + (y - k) % NY for z in zls])

    over_y(own, [zl])
    over_y(far, [zl ^ 4])
    pair = jnp.concatenate([own, far], axis=0)
    for k in (1, 3, 2):
        got = lax.ppermute(pair, "zl", [(i, (i & 4) | ((i + k) & 3)) for i in range(8)])
        z = (zl & 4) | ((zl - k) & 3)
        over_y(got, [z, z ^ 4])

    ws, wk = [], []
    for block, h in ((w, zh), (other, 1 - zh)):
        for k in (0, 1, 3, 2):
            got = block if k == 0 else lax.ppermute(block, "x", shift(NX, k))
            ws.append(got)
            wk.append((x - k) % NX * 4 + h * 2 + co)
    for i in range(8):
        ws.append(lax.ppermute(ws[i], "co", shift(2, 1)))
        wk.append(wk[i] + 1 - 2 * co)

    parts = mlp(
        jnp.stack(wk).astype(jnp.int32),
        jnp.stack(xr).astype(jnp.int32),
        ws,
        xs,
        tuple(xplan),
        in_project,
    )
    cot = jnp.concatenate([train_cotangent[0], roll_cotangent[0]], axis=0)
    right = jnp.dot(cot, out_project, preferred_element_type=jnp.float32).reshape(2, 8, RANK)
    lengths = jnp.stack([train_lengths, roll_lengths])
    live = (jnp.arange(8, dtype=jnp.int32)[None, :] < lengths).astype(jnp.float32)[:, :, None]
    live = jnp.broadcast_to(live, (2, 8, RANK))

    parts = lax.all_to_all(parts, ("zl", "y"), 0, 0, tiled=True)
    small = jax.ShapeDtypeStruct((8, 2 * RANK), jnp.float32)
    train, roll = pl.pallas_call(norm_kernel, out_shape=(small, small), name="norm")(
        parts, right, live
    )
    train_all = lax.all_to_all(
        jnp.broadcast_to(train, (32, 8, 2 * RANK)), ("zl", "y"), 0, 0, tiled=True
    )
    roll_all = lax.all_to_all(
        jnp.broadcast_to(roll, (16, 8, 2 * RANK)), ("x", "zh", "co"), 0, 0, tiled=True
    )
    return pl.pallas_call(
        score_kernel, out_shape=jax.ShapeDtypeStruct((32, 16), jnp.float32), name="score"
    )(train_all, roll_all)


def solution(mesh):
    fine = Mesh(mesh.devices.reshape(NX, NZH, NCO, NZL, NY), ("x", "zh", "co", "zl", "y"))
    rows, cols = ("x", "zh", "co"), ("zl", "y")
    placed = (
        P(rows + cols, None, None),
        P(rows + cols, None, None),
        P(rows + cols),
        P(cols + rows, None, None),
        P(cols + rows, None, None),
        P(cols + rows),
        P(rows, cols),
        P(rows, cols),
        P(cols, None),
        P(),
    )
    return jax.shard_map(
        on_device, mesh=fine, in_specs=placed, out_specs=P(rows, cols), check_vma=False
    )
```

```python
import functools

import jax
import jax.numpy as jnp
from jax import lax
from jax.experimental import pallas as pl
from jax.experimental.pallas import tpu as pltpu
from jax.sharding import Mesh, PartitionSpec as P

RANK = 64
NX, NZH, NCO, NZL, NY = 4, 2, 2, 8, 4
HIGH = lax.Precision.HIGHEST


def mlp_kernel(nx, nw, cols_ref, slot_ref, *refs):
    x_refs = refs[:nx]
    w_refs = refs[nx : nx + nw]
    ip_ref, out_ref, xv, wv, acc, xsem, wsem = refs[nx + nw :]
    copies, at = [], 0
    for i, x_ref in enumerate(x_refs):
        n = x_ref.shape[0]
        copies.append(pltpu.make_async_copy(x_ref, xv.at[pl.ds(at, n)], xsem.at[i]))
        at += n
    loads = [pltpu.make_async_copy(w_refs[p], wv.at[p], wsem.at[p]) for p in range(nw)]
    for c in copies:
        c.start()
    for c in loads:
        c.start()
    for c in copies:
        c.wait()
    for p in range(nw):
        loads[p].wait()
        picked = []
        for j in range(4):
            col = pl.multiple_of(cols_ref[p * 4 + j] * 256, 256)
            picked.append(xv[:, pl.ds(col, 256)])
        part = jnp.dot(
            jnp.concatenate(picked, axis=1),
            wv[p].reshape(1024, wv.shape[3]),
            preferred_element_type=jnp.float32,
        )
        if p == 0:
            acc[...] = part
        else:
            acc[...] += part
    half = acc.shape[1] // 2
    for m in range(4):
        rows = acc[m * 128 : (m + 1) * 128, :]
        gate, up = rows[:, :half], rows[:, half:]
        act = (gate / (1.0 + jnp.exp(-gate)) * up).astype(jnp.bfloat16)
        left = jnp.dot(act, ip_ref[...], preferred_element_type=jnp.float32)
        left = left.reshape(8, 2, 8, RANK)
        left = jnp.concatenate([left[:, 0], left[:, 1]], axis=-1)
        for i in range(8):
            out_ref[slot_ref[m * 8 + i]] = left[i]


def mlp(cols, slots, xs, ws, ip):
    any_ = pl.BlockSpec(memory_space=pl.ANY)
    smem = pl.BlockSpec(memory_space=pltpu.SMEM)
    nx, nw = len(xs), len(ws)
    return pl.pallas_call(
        functools.partial(mlp_kernel, nx, nw),
        out_shape=jax.ShapeDtypeStruct((32, 8, 2 * RANK), jnp.float32),
        in_specs=[smem, smem] + [any_] * (nx + nw) + [pl.BlockSpec(memory_space=pltpu.VMEM)],
        out_specs=pl.BlockSpec(memory_space=pltpu.VMEM),
        scratch_shapes=[
            pltpu.VMEM((512, xs[0].shape[1]), jnp.bfloat16),
            pltpu.VMEM((nw,) + ws[0].shape, jnp.bfloat16),
            pltpu.VMEM((512, ws[0].shape[2]), jnp.float32),
            pltpu.SemaphoreType.DMA((nx,)),
            pltpu.SemaphoreType.DMA((nw,)),
        ],
        compiler_params=pltpu.CompilerParams(vmem_limit_bytes=60 << 20),
        name="mlp",
    )(cols, slots, *xs, *ws, ip)


def norm_kernel(parts_ref, right_ref, live_ref, train_ref, roll_ref):
    left = jnp.sum(parts_ref[...], axis=0)
    for s, ref in ((0, train_ref), (1, roll_ref)):
        one = left[:, s * RANK : (s + 1) * RANK] * live_ref[s]
        right = right_ref[s]
        grad = lax.dot_general(
            one, right, (((0,), (0,)), ((), ())), precision=HIGH, preferred_element_type=jnp.float32
        )
        mean = jnp.sum(grad * grad) / (RANK * RANK)
        inv = 1.0 / jnp.sqrt(jnp.full((8, RANK), mean + 1e-6))
        ref[...] = jnp.concatenate([one * inv, right], axis=-1)


def score_kernel(train_ref, roll_ref, out_ref):
    t = train_ref[...].reshape(-1, 2 * RANK)
    r = roll_ref[...].reshape(-1, 2 * RANK)
    dims = (((1,), (1,)), ((), ()))
    a = lax.dot_general(
        t[:, :RANK], r[:, :RANK], dims, precision=HIGH, preferred_element_type=jnp.float32
    )
    b = lax.dot_general(
        t[:, RANK:], r[:, RANK:], dims, precision=HIGH, preferred_element_type=jnp.float32
    )
    both = jnp.sum((a * b).reshape(32, 8, 128), axis=1)
    pick = (
        lax.broadcasted_iota(jnp.int32, (128, 16), 0) // 8
        == lax.broadcasted_iota(jnp.int32, (128, 16), 1)
    ).astype(jnp.float32)
    out_ref[...] = jnp.dot(both, pick, precision=HIGH, preferred_element_type=jnp.float32) / RANK


def shift(n, k):
    return [(i, (i + k) % n) for i in range(n)]


def on_device(
    train_hidden,
    train_cotangent,
    train_lengths,
    roll_hidden,
    roll_cotangent,
    roll_lengths,
    gate_weight,
    up_weight,
    in_project,
    out_project,
):
    x, zh, co, zl, y = (lax.axis_index(a) for a in ("x", "zh", "co", "zl", "y"))
    width = train_hidden.shape[2]
    own = jnp.concatenate([train_hidden[0], roll_hidden[0]], axis=0)
    w = jnp.concatenate([gate_weight, up_weight], axis=1)

    other = lax.ppermute(w, "zh", shift(2, 1))

    block, zls = own, [zl]
    for k in (4, 2):
        got = lax.ppermute(block, "zl", [(i, i ^ k) for i in range(NZL)])
        block, zls = jnp.concatenate([block, got], axis=0), zls + [z ^ k for z in zls]
    twin = lax.ppermute(block, "zl", [(i, i ^ 1) for i in range(NZL)])

    first, second = [1, 0, 3, 2], [3, 2, 1, 0]
    step1 = [(c * NY + i, c * NY + (first, second)[c][i]) for c in range(2) for i in range(NY)]
    step2 = [(c * NY + i, c * NY + (second, first)[c][i]) for c in range(2) for i in range(NY)]
    y1 = jnp.where(co == 0, y ^ 1, 3 - y)
    y2 = jnp.where(co == 0, 3 - y, y ^ 1)
    y3 = y ^ 2
    xs, slots = [], []
    for part, at in ((block, zls), (twin, [z ^ 1 for z in zls])):
        got = lax.ppermute(part, ("co", "y"), step1)
        both = jnp.concatenate([part, got], axis=0)
        xs += [both, lax.ppermute(both, ("co", "y"), step2)]
        slots += [z * NY + o for o in (y, y1, y2, y3) for z in at]

    def over_x(a):
        spread = jnp.broadcast_to(a, (NX,) + a.shape)
        return lax.all_to_all(spread, "x", 0, 0, tiled=True)

    ws, cols = [], []
    for a, h in ((w, zh), (other, 1 - zh)):
        a = over_x(a)
        ws += [a, lax.ppermute(a, "co", shift(2, 1))]
        cols += [i * 4 + h * 2 + c for c in (co, 1 - co) for i in range(NX)]

    parts = mlp(
        jnp.stack(cols).astype(jnp.int32), jnp.stack(slots).astype(jnp.int32), xs, ws, in_project
    )
    cot = jnp.concatenate([train_cotangent[0], roll_cotangent[0]], axis=0)
    right = jnp.dot(cot, out_project, preferred_element_type=jnp.float32).reshape(2, 8, RANK)
    lengths = jnp.stack([train_lengths, roll_lengths])
    live = (jnp.arange(8, dtype=jnp.int32)[None, :] < lengths).astype(jnp.float32)[:, :, None]
    live = jnp.broadcast_to(live, (2, 8, RANK))

    parts = lax.all_to_all(parts, ("zl", "y"), 0, 0, tiled=True)
    small = jax.ShapeDtypeStruct((8, 2 * RANK), jnp.float32)
    train, roll = pl.pallas_call(norm_kernel, out_shape=(small, small), name="norm")(
        parts, right, live
    )
    far = lax.ppermute(roll, "zh", shift(2, 1))
    train_all = lax.all_to_all(
        jnp.broadcast_to(train, (32, 8, 2 * RANK)), ("zl", "y"), 0, 0, tiled=True
    )
    pair = jnp.where(zh == 0, jnp.stack([roll, far]), jnp.stack([far, roll]))
    roll_all = lax.all_to_all(
        jnp.broadcast_to(pair, (8, 2, 8, 2 * RANK)), ("x", "co"), 0, 0, tiled=True
    )
    roll_all = roll_all.reshape(NX, NCO, NZH, 8, 2 * RANK).transpose(0, 2, 1, 3, 4)
    roll_all = roll_all.reshape(16, 8, 2 * RANK)
    return pl.pallas_call(
        score_kernel, out_shape=jax.ShapeDtypeStruct((32, 16), jnp.float32), name="score"
    )(train_all, roll_all)


def solution(mesh):
    fine = Mesh(mesh.devices.reshape(NX, NZH, NCO, NZL, NY), ("x", "zh", "co", "zl", "y"))
    rows, cols = ("x", "zh", "co"), ("zl", "y")
    placed = (
        P(rows + cols, None, None),
        P(rows + cols, None, None),
        P(rows + cols),
        P(cols + rows, None, None),
        P(cols + rows, None, None),
        P(cols + rows),
        P(rows, cols),
        P(rows, cols),
        P(cols, None),
        P(),
    )
    return jax.shard_map(
        on_device, mesh=fine, in_specs=placed, out_specs=P(rows, cols), check_vma=False
    )
```

```python
import functools

import jax
import jax.numpy as jnp
from jax import lax
from jax.experimental import pallas as pl
from jax.experimental.pallas import tpu as pltpu
from jax.sharding import Mesh, PartitionSpec as P

RANK = 64
NX, NZH, NCO, NZL, NY = 4, 2, 2, 8, 4
HIGH = lax.Precision.HIGHEST


def mlp_kernel(nx, nw, cols_ref, slot_ref, *refs):
    x_refs = refs[:nx]
    w_refs = refs[nx : nx + nw]
    ip_ref, out_ref, xv, wv, acc, xsem, wsem = refs[nx + nw :]
    copies, at = [], 0
    for i, x_ref in enumerate(x_refs):
        n = x_ref.shape[0]
        copies.append(pltpu.make_async_copy(x_ref, xv.at[pl.ds(at, n)], xsem.at[i]))
        at += n
    loads, at = [], 0
    for p, w_ref in enumerate(w_refs):
        depth = w_ref.shape[1]
        loads.append((pltpu.make_async_copy(w_ref, wv.at[pl.ds(at, 4), pl.ds(0, depth)], wsem.at[p]), at, depth))
        at += 4
    for c in copies:
        c.start()
    for c, _, _ in loads:
        c.start()
    for c in copies:
        c.wait()
    for p, (c, at, depth) in enumerate(loads):
        c.wait()
        picked = []
        for j in range(4):
            col = pl.multiple_of(cols_ref[p * 4 + j], 128)
            picked.append(xv[:, pl.ds(col, depth)])
        part = jnp.dot(
            jnp.concatenate(picked, axis=1),
            wv[at : at + 4, :depth].reshape(4 * depth, wv.shape[2]),
            preferred_element_type=jnp.float32,
        )
        if p == 0:
            acc[...] = part
        else:
            acc[...] += part
    half = acc.shape[1] // 2
    for m in range(4):
        rows = acc[m * 128 : (m + 1) * 128, :]
        gate, up = rows[:, :half], rows[:, half:]
        act = (gate / (1.0 + jnp.exp(-gate)) * up).astype(jnp.bfloat16)
        left = jnp.dot(act, ip_ref[...], preferred_element_type=jnp.float32)
        left = left.reshape(8, 2, 8, RANK)
        left = jnp.concatenate([left[:, 0], left[:, 1]], axis=-1)
        for i in range(8):
            out_ref[slot_ref[m * 8 + i]] = left[i]


def mlp(cols, slots, xs, ws, ip):
    any_ = pl.BlockSpec(memory_space=pl.ANY)
    smem = pl.BlockSpec(memory_space=pltpu.SMEM)
    nx, nw = len(xs), len(ws)
    return pl.pallas_call(
        functools.partial(mlp_kernel, nx, nw),
        out_shape=jax.ShapeDtypeStruct((32, 8, 2 * RANK), jnp.float32),
        in_specs=[smem, smem] + [any_] * (nx + nw) + [pl.BlockSpec(memory_space=pltpu.VMEM)],
        out_specs=pl.BlockSpec(memory_space=pltpu.VMEM),
        scratch_shapes=[
            pltpu.VMEM((512, xs[0].shape[1]), jnp.bfloat16),
            pltpu.VMEM((4 * nw,) + ws[0].shape[1:], jnp.bfloat16),
            pltpu.VMEM((512, ws[0].shape[2]), jnp.float32),
            pltpu.SemaphoreType.DMA((nx,)),
            pltpu.SemaphoreType.DMA((nw,)),
        ],
        compiler_params=pltpu.CompilerParams(vmem_limit_bytes=60 << 20),
        name="mlp",
    )(cols, slots, *xs, *ws, ip)


def norm_kernel(parts_ref, right_ref, live_ref, train_ref, roll_ref):
    left = jnp.sum(parts_ref[...], axis=0)
    for s, ref in ((0, train_ref), (1, roll_ref)):
        one = left[:, s * RANK : (s + 1) * RANK] * live_ref[s]
        right = right_ref[s]
        grad = lax.dot_general(
            one, right, (((0,), (0,)), ((), ())), precision=HIGH, preferred_element_type=jnp.float32
        )
        mean = jnp.sum(grad * grad) / (RANK * RANK)
        inv = 1.0 / jnp.sqrt(jnp.full((8, RANK), mean + 1e-6))
        ref[...] = jnp.concatenate([one * inv, right], axis=-1)


def score_kernel(train_ref, roll_ref, out_ref):
    t = train_ref[...].reshape(-1, 2 * RANK)
    r = roll_ref[...].reshape(-1, 2 * RANK)
    dims = (((1,), (1,)), ((), ()))
    a = lax.dot_general(
        t[:, :RANK], r[:, :RANK], dims, precision=HIGH, preferred_element_type=jnp.float32
    )
    b = lax.dot_general(
        t[:, RANK:], r[:, RANK:], dims, precision=HIGH, preferred_element_type=jnp.float32
    )
    both = jnp.sum((a * b).reshape(32, 8, 128), axis=1)
    pick = (
        lax.broadcasted_iota(jnp.int32, (128, 16), 0) // 8
        == lax.broadcasted_iota(jnp.int32, (128, 16), 1)
    ).astype(jnp.float32)
    out_ref[...] = jnp.dot(both, pick, precision=HIGH, preferred_element_type=jnp.float32) / RANK


def shift(n, k):
    return [(i, (i + k) % n) for i in range(n)]


def on_device(
    train_hidden,
    train_cotangent,
    train_lengths,
    roll_hidden,
    roll_cotangent,
    roll_lengths,
    gate_weight,
    up_weight,
    in_project,
    out_project,
):
    x, zh, co, zl, y = (lax.axis_index(a) for a in ("x", "zh", "co", "zl", "y"))
    width = train_hidden.shape[2]
    own = jnp.concatenate([train_hidden[0], roll_hidden[0]], axis=0)
    w = jnp.concatenate([gate_weight, up_weight], axis=1)

    block, zls = own, [zl]
    for k in (4, 2):
        got = lax.ppermute(block, "zl", [(i, i ^ k) for i in range(NZL)])
        block, zls = jnp.concatenate([block, got], axis=0), zls + [z ^ k for z in zls]
    twin = lax.ppermute(block, "zl", [(i, i ^ 1) for i in range(NZL)])

    far_w, _ = lax.optimization_barrier((w, got))
    others = [lax.ppermute(far_w[:128], "zh", shift(2, 1))]
    far_w, _ = lax.optimization_barrier((far_w, twin))
    others.append(lax.ppermute(far_w[128:], "zh", shift(2, 1)))

    first, second = [1, 0, 3, 2], [3, 2, 1, 0]
    step1 = [(c * NY + i, c * NY + (first, second)[c][i]) for c in range(2) for i in range(NY)]
    step2 = [(c * NY + i, c * NY + (second, first)[c][i]) for c in range(2) for i in range(NY)]
    y1 = jnp.where(co == 0, y ^ 1, 3 - y)
    y2 = jnp.where(co == 0, 3 - y, y ^ 1)
    y3 = y ^ 2
    xs, slots = [], []
    for part, at in ((block, zls), (twin, [z ^ 1 for z in zls])):
        got = lax.ppermute(part, ("co", "y"), step1)
        both = jnp.concatenate([part, got], axis=0)
        xs += [both, lax.ppermute(both, ("co", "y"), step2)]
        slots += [z * NY + o for o in (y, y1, y2, y3) for z in at]

    def over_x(a):
        spread = jnp.broadcast_to(a, (NX,) + a.shape)
        return lax.all_to_all(spread, "x", 0, 0, tiled=True)

    ws, cols = [], []
    starts = [(i * 4 + zh * 2) * 256 for i in range(NX)]
    a = over_x(w)
    ws += [a, lax.ppermute(a, "co", shift(2, 1))]
    cols += [s + c * 256 for c in (co, 1 - co) for s in starts]
    starts = [(i * 4 + (1 - zh) * 2) * 256 for i in range(NX)]
    others[0], _ = lax.optimization_barrier((others[0], got))
    for half, other in enumerate(others):
        a = over_x(other)
        ws += [a, lax.ppermute(a, "co", shift(2, 1))]
        cols += [s + c * 256 + half * 128 for c in (co, 1 - co) for s in starts]

    parts = mlp(
        jnp.stack(cols).astype(jnp.int32), jnp.stack(slots).astype(jnp.int32), xs, ws, in_project
    )
    cot = jnp.concatenate([train_cotangent[0], roll_cotangent[0]], axis=0)
    right = jnp.dot(cot, out_project, preferred_element_type=jnp.float32).reshape(2, 8, RANK)
    lengths = jnp.stack([train_lengths, roll_lengths])
    live = (jnp.arange(8, dtype=jnp.int32)[None, :] < lengths).astype(jnp.float32)[:, :, None]
    live = jnp.broadcast_to(live, (2, 8, RANK))

    parts = lax.all_to_all(parts, ("zl", "y"), 0, 0, tiled=True)
    small = jax.ShapeDtypeStruct((8, 2 * RANK), jnp.float32)
    train, roll = pl.pallas_call(norm_kernel, out_shape=(small, small), name="norm")(
        parts, right, live
    )
    roll_all = lax.all_to_all(
        jnp.broadcast_to(roll, (16, 8, 2 * RANK)), ("x", "zh", "co"), 0, 0, tiled=True
    )
    train_all = lax.all_to_all(
        jnp.broadcast_to(train, (32, 8, 2 * RANK)), ("zl", "y"), 0, 0, tiled=True
    )
    return pl.pallas_call(
        score_kernel, out_shape=jax.ShapeDtypeStruct((32, 16), jnp.float32), name="score"
    )(train_all, roll_all)


def solution(mesh):
    fine = Mesh(mesh.devices.reshape(NX, NZH, NCO, NZL, NY), ("x", "zh", "co", "zl", "y"))
    rows, cols = ("x", "zh", "co"), ("zl", "y")
    placed = (
        P(rows + cols, None, None),
        P(rows + cols, None, None),
        P(rows + cols),
        P(cols + rows, None, None),
        P(cols + rows, None, None),
        P(cols + rows),
        P(rows, cols),
        P(rows, cols),
        P(cols, None),
        P(),
    )
    return jax.shard_map(
        on_device, mesh=fine, in_specs=placed, out_specs=P(rows, cols), check_vma=False
    )
```

```python
import functools

import jax
import jax.numpy as jnp
from jax import lax
from jax.experimental import pallas as pl
from jax.experimental.pallas import tpu as pltpu
from jax.sharding import Mesh, PartitionSpec as P

RANK = 64
NX, NZH, NCO, NZL, NY = 4, 2, 2, 8, 4
HIGH = lax.Precision.HIGHEST


def mlp_kernel(nx, nw, cols_ref, slot_ref, *refs):
    x_refs = refs[:nx]
    w_refs = refs[nx : nx + nw]
    ip_ref, out_ref, xv, wv, acc, xsem, wsem = refs[nx + nw :]
    copies, at = [], 0
    for i, x_ref in enumerate(x_refs):
        n = x_ref.shape[0]
        copies.append(pltpu.make_async_copy(x_ref, xv.at[pl.ds(at, n)], xsem.at[i]))
        at += n
    loads, at = [], 0
    for p, w_ref in enumerate(w_refs):
        depth = w_ref.shape[1]
        loads.append((pltpu.make_async_copy(w_ref, wv.at[pl.ds(at, 4), pl.ds(0, depth)], wsem.at[p]), at, depth))
        at += 4
    for c in copies:
        c.start()
    for c, _, _ in loads:
        c.start()
    for c in copies:
        c.wait()
    for p, (c, at, depth) in enumerate(loads):
        c.wait()
        picked = []
        for j in range(4):
            col = pl.multiple_of(cols_ref[p * 4 + j], 128)
            picked.append(xv[:, pl.ds(col, depth)])
        part = jnp.dot(
            jnp.concatenate(picked, axis=1),
            wv[at : at + 4, :depth].reshape(4 * depth, wv.shape[2]),
            preferred_element_type=jnp.float32,
        )
        if p == 0:
            acc[...] = part
        else:
            acc[...] += part
    half = acc.shape[1] // 2
    for m in range(4):
        rows = acc[m * 128 : (m + 1) * 128, :]
        gate, up = rows[:, :half], rows[:, half:]
        act = (gate / (1.0 + jnp.exp(-gate)) * up).astype(jnp.bfloat16)
        left = lax.dot_general(
            act, ip_ref[...], (((1,), (1,)), ((), ())), preferred_element_type=jnp.float32
        )
        left = left.reshape(8, 2, 8, RANK)
        left = jnp.concatenate([left[:, 0], left[:, 1]], axis=-1)
        for i in range(8):
            out_ref[slot_ref[m * 8 + i]] = left[i]


def mlp(cols, slots, xs, ws, ip):
    any_ = pl.BlockSpec(memory_space=pl.ANY)
    smem = pl.BlockSpec(memory_space=pltpu.SMEM)
    nx, nw = len(xs), len(ws)
    return pl.pallas_call(
        functools.partial(mlp_kernel, nx, nw),
        out_shape=jax.ShapeDtypeStruct((32, 8, 2 * RANK), jnp.float32),
        in_specs=[smem, smem] + [any_] * (nx + nw) + [pl.BlockSpec(memory_space=pltpu.VMEM)],
        out_specs=pl.BlockSpec(memory_space=pltpu.VMEM),
        scratch_shapes=[
            pltpu.VMEM((512, xs[0].shape[1]), jnp.bfloat16),
            pltpu.VMEM((4 * nw,) + ws[0].shape[1:], jnp.bfloat16),
            pltpu.VMEM((512, ws[0].shape[2]), jnp.float32),
            pltpu.SemaphoreType.DMA((nx,)),
            pltpu.SemaphoreType.DMA((nw,)),
        ],
        compiler_params=pltpu.CompilerParams(vmem_limit_bytes=60 << 20),
        name="mlp",
    )(cols, slots, *xs, *ws, ip)


def norm_kernel(parts_ref, right_ref, train_len_ref, roll_len_ref, train_ref, roll_ref):
    left = jnp.sum(parts_ref[...], axis=0)
    token = lax.broadcasted_iota(jnp.int32, (8, RANK), 0)
    for s, (len_ref, ref) in enumerate(((train_len_ref, train_ref), (roll_len_ref, roll_ref))):
        one = jnp.where(token < len_ref[0], left[:, s * RANK : (s + 1) * RANK], 0.0)
        right = right_ref[s]
        grad = lax.dot_general(
            one, right, (((0,), (0,)), ((), ())), precision=HIGH, preferred_element_type=jnp.float32
        )
        mean = jnp.sum(grad * grad) / (RANK * RANK)
        inv = 1.0 / jnp.sqrt(jnp.full((8, RANK), mean + 1e-6))
        ref[...] = jnp.concatenate([one * inv, right], axis=-1)


def score_kernel(train_ref, roll_ref, out_ref):
    t = train_ref[...].reshape(-1, 2 * RANK)
    r = roll_ref[...].reshape(-1, 2 * RANK)
    dims = (((1,), (1,)), ((), ()))
    a = lax.dot_general(
        r[:, :RANK], t[:, :RANK], dims, precision=HIGH, preferred_element_type=jnp.float32
    )
    b = lax.dot_general(
        r[:, RANK:], t[:, RANK:], dims, precision=HIGH, preferred_element_type=jnp.float32
    )
    both = jnp.sum((a * b).reshape(16, 8, 256), axis=1)
    pick = (
        lax.broadcasted_iota(jnp.int32, (256, 32), 0) // 8
        == lax.broadcasted_iota(jnp.int32, (256, 32), 1)
    ).astype(jnp.float32)
    out_ref[...] = jnp.dot(both, pick, precision=HIGH, preferred_element_type=jnp.float32) / RANK


def shift(n, k):
    return [(i, (i + k) % n) for i in range(n)]


def on_device(
    train_hidden,
    train_cotangent,
    train_lengths,
    roll_hidden,
    roll_cotangent,
    roll_lengths,
    gate_weight,
    up_weight,
    in_project,
    out_project,
):
    x, zh, co, zl, y = (lax.axis_index(a) for a in ("x", "zh", "co", "zl", "y"))
    width = train_hidden.shape[2]
    own = jnp.concatenate([train_hidden[0], roll_hidden[0]], axis=0)
    w = jnp.concatenate([gate_weight, up_weight], axis=1)

    block, zls = own, [zl]
    for k in (4, 2):
        got = lax.ppermute(block, "zl", [(i, i ^ k) for i in range(NZL)])
        if k == 4:
            far_w, _ = lax.optimization_barrier((w, got))
            other = lax.ppermute(far_w, "zh", shift(2, 1))
        block, zls = jnp.concatenate([block, got], axis=0), zls + [z ^ k for z in zls]
    twin = lax.ppermute(block, "zl", [(i, i ^ 1) for i in range(NZL)])

    first, second = [1, 0, 3, 2], [3, 2, 1, 0]
    step1 = [(c * NY + i, c * NY + (first, second)[c][i]) for c in range(2) for i in range(NY)]
    step2 = [(c * NY + i, c * NY + (second, first)[c][i]) for c in range(2) for i in range(NY)]
    y1 = jnp.where(co == 0, y ^ 1, 3 - y)
    y2 = jnp.where(co == 0, 3 - y, y ^ 1)
    y3 = y ^ 2
    xs, slots = [], []
    for part, at in ((block, zls), (twin, [z ^ 1 for z in zls])):
        got = lax.ppermute(part, ("co", "y"), step1)
        both = jnp.concatenate([part, got], axis=0)
        xs += [both, lax.ppermute(both, ("co", "y"), step2)]
        slots += [z * NY + o for o in (y, y1, y2, y3) for z in at]

    def over_x(a):
        spread = jnp.broadcast_to(a, (NX,) + a.shape)
        return lax.all_to_all(spread, "x", 0, 0, tiled=True)

    ws, cols = [], []
    other, _ = lax.optimization_barrier((other, got))
    for a, h in ((w, zh), (other, 1 - zh)):
        a = over_x(a)
        ws += [a, lax.ppermute(a, "co", shift(2, 1))]
        cols += [(i * 4 + h * 2 + c) * 256 for c in (co, 1 - co) for i in range(NX)]

    parts = mlp(
        jnp.stack(cols).astype(jnp.int32), jnp.stack(slots).astype(jnp.int32), xs, ws, in_project.T
    )
    cot = jnp.concatenate([train_cotangent[0], roll_cotangent[0]], axis=0)
    right = jnp.dot(cot, out_project, preferred_element_type=jnp.float32).reshape(2, 8, RANK)
    parts = lax.all_to_all(parts, ("zl", "y"), 0, 0, tiled=True)
    small = jax.ShapeDtypeStruct((8, 2 * RANK), jnp.float32)
    vmem, smem = pl.BlockSpec(memory_space=pltpu.VMEM), pl.BlockSpec(memory_space=pltpu.SMEM)
    train, roll = pl.pallas_call(
        norm_kernel, out_shape=(small, small), in_specs=[vmem, vmem, smem, smem], name="norm"
    )(parts, right, train_lengths, roll_lengths)
    roll_all = lax.all_to_all(
        jnp.broadcast_to(roll, (16, 8, 2 * RANK)), ("x", "zh", "co"), 0, 0, tiled=True
    )
    train_all = lax.all_to_all(
        jnp.broadcast_to(train, (32, 8, 2 * RANK)), ("zl", "y"), 0, 0, tiled=True
    )
    scores = pl.pallas_call(
        score_kernel, out_shape=jax.ShapeDtypeStruct((16, 32), jnp.float32), name="score"
    )(train_all, roll_all)
    return scores.T


def solution(mesh):
    fine = Mesh(mesh.devices.reshape(NX, NZH, NCO, NZL, NY), ("x", "zh", "co", "zl", "y"))
    rows, cols = ("x", "zh", "co"), ("zl", "y")
    placed = (
        P(rows + cols, None, None),
        P(rows + cols, None, None),
        P(rows + cols),
        P(cols + rows, None, None),
        P(cols + rows, None, None),
        P(cols + rows),
        P(rows, cols),
        P(rows, cols),
        P(cols, None),
        P(),
    )
    return jax.shard_map(
        on_device, mesh=fine, in_specs=placed, out_specs=P(rows, cols), check_vma=False
    )
```

```python
import functools

import jax
import jax.numpy as jnp
from jax import lax
from jax.experimental import pallas as pl
from jax.experimental.pallas import tpu as pltpu
from jax.sharding import Mesh, PartitionSpec as P

RANK = 64
NX, NZH, NCO, NZL, NY = 4, 2, 2, 8, 4
HIGH = lax.Precision.HIGHEST


def mlp_kernel(nx, nw, cols_ref, slot_ref, *refs):
    x_refs = refs[:nx]
    w_refs = refs[nx : nx + nw]
    ip_ref, out_ref, xv, wv, acc, xsem, wsem = refs[nx + nw :]
    half_k = xv.shape[1] // 2
    xcopies, wcopies = [[], []], [[], []]
    for h in range(2):
        at = 0
        for i, x_ref in enumerate(x_refs):
            n = x_ref.shape[0]
            cut = pl.ds(h * half_k, half_k)
            xcopies[h].append(
                pltpu.make_async_copy(x_ref.at[:, cut], xv.at[pl.ds(at, n), cut], xsem.at[h * nx + i])
            )
            at += n
    for p in range(nw):
        for j in range(4):
            row = pl.multiple_of(cols_ref[p * 4 + j], 256)
            wcopies[j // 2].append(
                pltpu.make_async_copy(w_refs[p].at[j], wv.at[pl.ds(row, 256)], wsem.at[p * 4 + j])
            )
    for h in range(2):
        for c in xcopies[h] + wcopies[h]:
            c.start()
    for c in xcopies[0] + wcopies[0]:
        c.wait()
    acc[...] = jnp.dot(xv[:, :half_k], wv[:half_k], preferred_element_type=jnp.float32)
    for c in xcopies[1] + wcopies[1]:
        c.wait()
    acc[...] += jnp.dot(xv[:, half_k:], wv[half_k:], preferred_element_type=jnp.float32)
    half = acc.shape[1] // 2
    for m in range(4):
        both = acc[m * 128 : (m + 1) * 128]
        gate, up = both[:, :half], both[:, half:]
        act = (gate / (1.0 + jnp.exp(-gate)) * up).astype(jnp.bfloat16)
        left = lax.dot_general(
            act, ip_ref[...], (((1,), (1,)), ((), ())), preferred_element_type=jnp.float32
        )
        left = left.reshape(8, 2, 8, RANK)
        left = jnp.concatenate([left[:, 0], left[:, 1]], axis=-1)
        for i in range(8):
            out_ref[slot_ref[m * 8 + i]] = left[i]


def mlp(cols, slots, xs, ws, ip):
    any_ = pl.BlockSpec(memory_space=pl.ANY)
    smem = pl.BlockSpec(memory_space=pltpu.SMEM)
    nx, nw = len(xs), len(ws)
    return pl.pallas_call(
        functools.partial(mlp_kernel, nx, nw),
        out_shape=jax.ShapeDtypeStruct((32, 8, 2 * RANK), jnp.float32),
        in_specs=[smem, smem] + [any_] * (nx + nw) + [pl.BlockSpec(memory_space=pltpu.VMEM)],
        out_specs=pl.BlockSpec(memory_space=pltpu.VMEM),
        scratch_shapes=[
            pltpu.VMEM((512, xs[0].shape[1]), jnp.bfloat16),
            pltpu.VMEM((4096, ws[0].shape[2]), jnp.bfloat16),
            pltpu.VMEM((512, ws[0].shape[2]), jnp.float32),
            pltpu.SemaphoreType.DMA((2 * nx,)),
            pltpu.SemaphoreType.DMA((4 * nw,)),
        ],
        compiler_params=pltpu.CompilerParams(vmem_limit_bytes=60 << 20),
        name="mlp",
    )(cols, slots, *xs, *ws, ip)


def norm_kernel(parts_ref, right_ref, train_len_ref, roll_len_ref, train_ref, roll_ref):
    left = jnp.sum(parts_ref[...], axis=0)
    token = lax.broadcasted_iota(jnp.int32, (8, RANK), 0)
    for s, (len_ref, ref) in enumerate(((train_len_ref, train_ref), (roll_len_ref, roll_ref))):
        one = jnp.where(token < len_ref[0], left[:, s * RANK : (s + 1) * RANK], 0.0)
        right = right_ref[s]
        grad = lax.dot_general(
            one, right, (((0,), (0,)), ((), ())), precision=HIGH, preferred_element_type=jnp.float32
        )
        mean = jnp.sum(grad * grad) / (RANK * RANK)
        inv = 1.0 / jnp.sqrt(jnp.full((8, RANK), mean + 1e-6))
        ref[...] = jnp.concatenate([one * inv, right], axis=-1)


def score_kernel(train_ref, roll_ref, y_ref, out_ref):
    t = train_ref[...].reshape(-1, 2 * RANK)
    r = roll_ref[...].reshape(-1, 2 * RANK)
    dims = (((1,), (1,)), ((), ()))
    a = lax.dot_general(
        r[:, :RANK], t[:, :RANK], dims, precision=HIGH, preferred_element_type=jnp.float32
    )
    b = lax.dot_general(
        r[:, RANK:], t[:, RANK:], dims, precision=HIGH, preferred_element_type=jnp.float32
    )
    both = jnp.sum((a * b).reshape(16, 8, 256), axis=1)
    group = lax.broadcasted_iota(jnp.int32, (256, 32), 0) // 8
    step = group & 3
    step = step ^ (step >> 1)
    column = (group & 28) + ((y_ref[0] - step) & 3)
    pick = (column == lax.broadcasted_iota(jnp.int32, (256, 32), 1)).astype(jnp.float32)
    out_ref[...] = jnp.dot(both, pick, precision=HIGH, preferred_element_type=jnp.float32) / RANK


def shift(n, k):
    return [(i, (i + k) % n) for i in range(n)]


def on_device(
    train_hidden,
    train_cotangent,
    train_lengths,
    roll_hidden,
    roll_cotangent,
    roll_lengths,
    gate_weight,
    up_weight,
    in_project,
    out_project,
):
    x, zh, co, zl, y = (lax.axis_index(a) for a in ("x", "zh", "co", "zl", "y"))
    width = train_hidden.shape[2]
    own = jnp.concatenate([train_hidden[0], roll_hidden[0]], axis=0)
    w = jnp.concatenate([gate_weight, up_weight], axis=1)

    other = lax.ppermute(w, "zh", shift(2, 1))

    block, zls = own, [zl]
    for k in (4, 2):
        got = lax.ppermute(block, "zl", [(i, i ^ k) for i in range(NZL)])
        block, zls = jnp.concatenate([block, got], axis=0), zls + [z ^ k for z in zls]
    twin = lax.ppermute(block, "zl", [(i, i ^ 1) for i in range(NZL)])

    first, second = [1, 0, 3, 2], [3, 2, 1, 0]
    step1 = [(c * NY + i, c * NY + (first, second)[c][i]) for c in range(2) for i in range(NY)]
    step2 = [(c * NY + i, c * NY + (second, first)[c][i]) for c in range(2) for i in range(NY)]
    y1 = jnp.where(co == 0, y ^ 1, 3 - y)
    y2 = jnp.where(co == 0, 3 - y, y ^ 1)
    y3 = y ^ 2
    xs, slots = [], []
    for part, at in ((block, zls), (twin, [z ^ 1 for z in zls])):
        got = lax.ppermute(part, ("co", "y"), step1)
        both = jnp.concatenate([part, got], axis=0)
        xs += [both, lax.ppermute(both, ("co", "y"), step2)]
        slots += [z * NY + o for o in (y, y1, y2, y3) for z in at]

    def over_x(a):
        spread = jnp.broadcast_to(a, (NX,) + a.shape)
        return lax.all_to_all(spread, "x", 0, 0, tiled=True)

    ws, cols = [], []
    for a, h in ((w, zh), (other, 1 - zh)):
        a = over_x(a)
        ws += [a, lax.ppermute(a, "co", shift(2, 1))]
        cols += [(i * 4 + h * 2 + c) * 256 for c in (co, 1 - co) for i in range(NX)]

    parts = mlp(
        jnp.stack(cols).astype(jnp.int32), jnp.stack(slots).astype(jnp.int32), xs, ws, in_project.T
    )
    cot = jnp.concatenate([train_cotangent[0], roll_cotangent[0]], axis=0)
    right = jnp.dot(cot, out_project, preferred_element_type=jnp.float32).reshape(2, 8, RANK)
    parts = lax.all_to_all(parts, ("zl", "y"), 0, 0, tiled=True)
    small = jax.ShapeDtypeStruct((8, 2 * RANK), jnp.float32)
    vmem, smem = pl.BlockSpec(memory_space=pltpu.VMEM), pl.BlockSpec(memory_space=pltpu.SMEM)
    train, roll = pl.pallas_call(
        norm_kernel, out_shape=(small, small), in_specs=[vmem, vmem, smem, smem], name="norm"
    )(parts, right, train_lengths, roll_lengths)
    roll_all = lax.all_to_all(
        jnp.broadcast_to(roll, (16, 8, 2 * RANK)), ("x", "zh", "co"), 0, 0, tiled=True
    )
    near = [train] + [lax.ppermute(train, "y", shift(NY, k)) for k in (1, 3, 2)]
    train_all = lax.all_to_all(
        jnp.broadcast_to(jnp.stack(near), (NZL, NY, 8, 2 * RANK)), "zl", 0, 0, tiled=True
    )
    scores = pl.pallas_call(
        score_kernel,
        out_shape=jax.ShapeDtypeStruct((16, 32), jnp.float32),
        in_specs=[vmem, vmem, smem],
        name="score",
    )(train_all, roll_all, y.astype(jnp.int32).reshape(1))
    return scores.T


def solution(mesh):
    fine = Mesh(mesh.devices.reshape(NX, NZH, NCO, NZL, NY), ("x", "zh", "co", "zl", "y"))
    rows, cols = ("x", "zh", "co"), ("zl", "y")
    placed = (
        P(rows + cols, None, None),
        P(rows + cols, None, None),
        P(rows + cols),
        P(cols + rows, None, None),
        P(cols + rows, None, None),
        P(cols + rows),
        P(rows, cols),
        P(rows, cols),
        P(cols, None),
        P(),
    )
    return jax.shard_map(
        on_device, mesh=fine, in_specs=placed, out_specs=P(rows, cols), check_vma=False
    )
```

```python
import functools

import jax
import jax.numpy as jnp
from jax import lax
from jax.experimental import pallas as pl
from jax.experimental.pallas import tpu as pltpu
from jax.sharding import Mesh, PartitionSpec as P

RANK = 64
NX, NZH, NCO, NZL, NY = 4, 2, 2, 8, 4
HIGH = lax.Precision.HIGHEST


def mlp_kernel(nx, nw, cols_ref, slot_ref, *refs):
    x_refs = refs[:nx]
    w_refs = refs[nx : nx + nw]
    ip_ref, out_ref, xv, wv, acc, xsem, wsem = refs[nx + nw :]
    half_k = xv.shape[1] // 2
    xcopies, wcopies = [[], []], [[], []]
    for h in range(2):
        at = 0
        for i, x_ref in enumerate(x_refs):
            n = x_ref.shape[0]
            cut = pl.ds(h * half_k, half_k)
            xcopies[h].append(
                pltpu.make_async_copy(x_ref.at[:, cut], xv.at[pl.ds(at, n), cut], xsem.at[h * nx + i])
            )
            at += n
    for p in range(nw):
        for j in range(4):
            row = pl.multiple_of(cols_ref[p * 4 + j], 256)
            wcopies[j // 2].append(
                pltpu.make_async_copy(w_refs[p].at[j], wv.at[pl.ds(row, 256)], wsem.at[p * 4 + j])
            )
    for h in range(2):
        for c in xcopies[h] + wcopies[h]:
            c.start()
    for c in xcopies[0] + wcopies[0]:
        c.wait()
    acc[...] = jnp.dot(xv[:, :half_k], wv[:half_k], preferred_element_type=jnp.float32)
    for c in xcopies[1] + wcopies[1]:
        c.wait()
    acc[...] += jnp.dot(xv[:, half_k:], wv[half_k:], preferred_element_type=jnp.float32)
    half = acc.shape[1] // 2
    for m in range(4):
        both = acc[m * 128 : (m + 1) * 128]
        gate, up = both[:, :half], both[:, half:]
        act = (gate / (1.0 + jnp.exp(-gate)) * up).astype(jnp.bfloat16)
        left = lax.dot_general(
            act, ip_ref[...], (((1,), (1,)), ((), ())), preferred_element_type=jnp.float32
        )
        left = left.reshape(8, 2, 8, RANK)
        left = jnp.concatenate([left[:, 0], left[:, 1]], axis=-1)
        for i in range(8):
            out_ref[slot_ref[m * 8 + i]] = left[i]


def mlp(cols, slots, xs, ws, ip):
    any_ = pl.BlockSpec(memory_space=pl.ANY)
    smem = pl.BlockSpec(memory_space=pltpu.SMEM)
    nx, nw = len(xs), len(ws)
    return pl.pallas_call(
        functools.partial(mlp_kernel, nx, nw),
        out_shape=jax.ShapeDtypeStruct((32, 8, 2 * RANK), jnp.float32),
        in_specs=[smem, smem] + [any_] * (nx + nw) + [pl.BlockSpec(memory_space=pltpu.VMEM)],
        out_specs=pl.BlockSpec(memory_space=pltpu.VMEM),
        scratch_shapes=[
            pltpu.VMEM((512, xs[0].shape[1]), jnp.bfloat16),
            pltpu.VMEM((4096, ws[0].shape[2]), jnp.bfloat16),
            pltpu.VMEM((512, ws[0].shape[2]), jnp.float32),
            pltpu.SemaphoreType.DMA((2 * nx,)),
            pltpu.SemaphoreType.DMA((4 * nw,)),
        ],
        compiler_params=pltpu.CompilerParams(vmem_limit_bytes=60 << 20),
        name="mlp",
    )(cols, slots, *xs, *ws, ip)


def norm_kernel(parts_ref, right_ref, train_len_ref, roll_len_ref, train_ref, roll_ref):
    left = jnp.sum(parts_ref[...], axis=0)
    token = lax.broadcasted_iota(jnp.int32, (8, RANK), 0)
    for s, (len_ref, ref) in enumerate(((train_len_ref, train_ref), (roll_len_ref, roll_ref))):
        one = jnp.where(token < len_ref[0], left[:, s * RANK : (s + 1) * RANK], 0.0)
        right = right_ref[s]
        grad = lax.dot_general(
            one, right, (((0,), (0,)), ((), ())), precision=HIGH, preferred_element_type=jnp.float32
        )
        mean = jnp.sum(grad * grad) / (RANK * RANK)
        inv = 1.0 / jnp.sqrt(jnp.full((8, RANK), mean + 1e-6))
        ref[...] = jnp.broadcast_to(jnp.concatenate([one * inv, right], axis=-1), ref.shape)


def score_kernel(train_ref, roll_ref, y_ref, out_ref):
    t = train_ref[...].reshape(-1, 2 * RANK)
    r = roll_ref[...].reshape(-1, 2 * RANK)
    dims = (((1,), (1,)), ((), ()))
    a = lax.dot_general(
        r[:, :RANK], t[:, :RANK], dims, precision=HIGH, preferred_element_type=jnp.float32
    )
    b = lax.dot_general(
        r[:, RANK:], t[:, RANK:], dims, precision=HIGH, preferred_element_type=jnp.float32
    )
    both = jnp.sum((a * b).reshape(16, 8, 256), axis=1)
    group = lax.broadcasted_iota(jnp.int32, (256, 32), 0) // 8
    step = group & 3
    step = step ^ (step >> 1)
    column = (group & 28) + ((y_ref[0] - step) & 3)
    pick = (column == lax.broadcasted_iota(jnp.int32, (256, 32), 1)).astype(jnp.float32)
    out_ref[...] = jnp.dot(both, pick, precision=HIGH, preferred_element_type=jnp.float32) / RANK


def shift(n, k):
    return [(i, (i + k) % n) for i in range(n)]


def on_device(
    train_hidden,
    train_cotangent,
    train_lengths,
    roll_hidden,
    roll_cotangent,
    roll_lengths,
    gate_weight,
    up_weight,
    in_project,
    out_project,
):
    x, zh, co, zl, y = (lax.axis_index(a) for a in ("x", "zh", "co", "zl", "y"))
    width = train_hidden.shape[2]
    own = jnp.concatenate([train_hidden[0], roll_hidden[0]], axis=0)
    w = jnp.concatenate([gate_weight, up_weight], axis=1)

    other = lax.ppermute(w, "zh", shift(2, 1))

    block, zls = own, [zl]
    for k in (4, 2):
        got = lax.ppermute(block, "zl", [(i, i ^ k) for i in range(NZL)])
        block, zls = jnp.concatenate([block, got], axis=0), zls + [z ^ k for z in zls]
    twin = lax.ppermute(block, "zl", [(i, i ^ 1) for i in range(NZL)])

    first, second = [1, 0, 3, 2], [3, 2, 1, 0]
    step1 = [(c * NY + i, c * NY + (first, second)[c][i]) for c in range(2) for i in range(NY)]
    step2 = [(c * NY + i, c * NY + (second, first)[c][i]) for c in range(2) for i in range(NY)]
    y1 = jnp.where(co == 0, y ^ 1, 3 - y)
    y2 = jnp.where(co == 0, 3 - y, y ^ 1)
    y3 = y ^ 2
    xs, slots = [], []
    for part, at in ((block, zls), (twin, [z ^ 1 for z in zls])):
        got = lax.ppermute(part, ("co", "y"), step1)
        both = jnp.concatenate([part, got], axis=0)
        xs += [both, lax.ppermute(both, ("co", "y"), step2)]
        slots += [z * NY + o for o in (y, y1, y2, y3) for z in at]

    def over_x(a):
        spread = jnp.broadcast_to(a, (NX,) + a.shape)
        return lax.all_to_all(spread, "x", 0, 0, tiled=True)

    ws, cols = [], []
    for a, h in ((w, zh), (other, 1 - zh)):
        a = over_x(a)
        ws += [a, lax.ppermute(a, "co", shift(2, 1))]
        cols += [(i * 4 + h * 2 + c) * 256 for c in (co, 1 - co) for i in range(NX)]

    parts = mlp(
        jnp.stack(cols).astype(jnp.int32), jnp.stack(slots).astype(jnp.int32), xs, ws, in_project.T
    )
    cot = jnp.concatenate([train_cotangent[0], roll_cotangent[0]], axis=0)
    right = jnp.dot(cot, out_project, preferred_element_type=jnp.float32).reshape(2, 8, RANK)
    parts = lax.all_to_all(parts, ("zl", "y"), 0, 0, tiled=True)
    small = jax.ShapeDtypeStruct((8, 2 * RANK), jnp.float32)
    vmem, smem = pl.BlockSpec(memory_space=pltpu.VMEM), pl.BlockSpec(memory_space=pltpu.SMEM)
    train, roll = pl.pallas_call(
        norm_kernel,
        out_shape=[small, jax.ShapeDtypeStruct((16, 8, 2 * RANK), jnp.float32)],
        in_specs=[vmem, vmem, smem, smem],
        name="norm",
    )(parts, right, train_lengths, roll_lengths)
    roll_all = lax.all_to_all(
        roll, ("x", "zh", "co"), 0, 0, tiled=True
    )
    near = [train] + [lax.ppermute(train, "y", shift(NY, k)) for k in (1, 3, 2)]
    train_all = lax.all_to_all(
        jnp.broadcast_to(jnp.stack(near), (NZL, NY, 8, 2 * RANK)), "zl", 0, 0, tiled=True
    )
    scores = pl.pallas_call(
        score_kernel,
        out_shape=jax.ShapeDtypeStruct((16, 32), jnp.float32),
        in_specs=[vmem, vmem, smem],
        name="score",
    )(train_all, roll_all, y.astype(jnp.int32).reshape(1))
    return scores.T


def solution(mesh):
    fine = Mesh(mesh.devices.reshape(NX, NZH, NCO, NZL, NY), ("x", "zh", "co", "zl", "y"))
    rows, cols = ("x", "zh", "co"), ("zl", "y")
    placed = (
        P(rows + cols, None, None),
        P(rows + cols, None, None),
        P(rows + cols),
        P(cols + rows, None, None),
        P(cols + rows, None, None),
        P(cols + rows),
        P(rows, cols),
        P(rows, cols),
        P(cols, None),
        P(),
    )
    return jax.shard_map(
        on_device, mesh=fine, in_specs=placed, out_specs=P(rows, cols), check_vma=False
    )
```

```python
import functools

import jax
import jax.numpy as jnp
from jax import lax
from jax.experimental import pallas as pl
from jax.experimental.pallas import tpu as pltpu
from jax.sharding import Mesh, PartitionSpec as P

RANK = 64
NX, NZH, NCO, NZL, NY = 4, 2, 2, 8, 4
HIGH = lax.Precision.HIGHEST


def mlp_kernel(nx, nw, cols_ref, slot_ref, *refs):
    x_refs = refs[:nx]
    w_refs = refs[nx : nx + nw]
    ip_ref, out_ref, xv, wv, acc, xsem, wsem = refs[nx + nw :]
    part_k = xv.shape[1] // 4
    groups = []
    for h in range(4):
        at, copies = 0, []
        for i, x_ref in enumerate(x_refs):
            n = x_ref.shape[0]
            cut = pl.ds(h * part_k, part_k)
            copies.append(
                pltpu.make_async_copy(x_ref.at[:, cut], xv.at[pl.ds(at, n), cut], xsem.at[h * nx + i])
            )
            at += n
        for p in range(nw):
            row = pl.multiple_of(cols_ref[p * 4 + h], 256)
            copies.append(
                pltpu.make_async_copy(w_refs[p].at[h], wv.at[pl.ds(row, 256)], wsem.at[p * 4 + h])
            )
        groups.append(copies)
    for copies in groups:
        for c in copies:
            c.start()
    for h, copies in enumerate(groups):
        for c in copies:
            c.wait()
        k = slice(h * part_k, (h + 1) * part_k)
        part = jnp.dot(xv[:, k], wv[k], preferred_element_type=jnp.float32)
        if h:
            acc[...] += part
        else:
            acc[...] = part
    half = acc.shape[1] // 2
    for m in range(4):
        both = acc[m * 128 : (m + 1) * 128]
        gate, up = both[:, :half], both[:, half:]
        act = (gate / (1.0 + jnp.exp(-gate)) * up).astype(jnp.bfloat16)
        left = lax.dot_general(
            act, ip_ref[...], (((1,), (1,)), ((), ())), preferred_element_type=jnp.float32
        )
        left = left.reshape(8, 2, 8, RANK)
        left = jnp.concatenate([left[:, 0], left[:, 1]], axis=-1)
        for i in range(8):
            out_ref[slot_ref[m * 8 + i]] = left[i]


def mlp(cols, slots, xs, ws, ip):
    any_ = pl.BlockSpec(memory_space=pl.ANY)
    smem = pl.BlockSpec(memory_space=pltpu.SMEM)
    nx, nw = len(xs), len(ws)
    return pl.pallas_call(
        functools.partial(mlp_kernel, nx, nw),
        out_shape=jax.ShapeDtypeStruct((32, 8, 2 * RANK), jnp.float32),
        in_specs=[smem, smem] + [any_] * (nx + nw) + [pl.BlockSpec(memory_space=pltpu.VMEM)],
        out_specs=pl.BlockSpec(memory_space=pltpu.VMEM),
        scratch_shapes=[
            pltpu.VMEM((512, xs[0].shape[1]), jnp.bfloat16),
            pltpu.VMEM((4096, ws[0].shape[2]), jnp.bfloat16),
            pltpu.VMEM((512, ws[0].shape[2]), jnp.float32),
            pltpu.SemaphoreType.DMA((4 * nx,)),
            pltpu.SemaphoreType.DMA((4 * nw,)),
        ],
        compiler_params=pltpu.CompilerParams(vmem_limit_bytes=60 << 20),
        name="mlp",
    )(cols, slots, *xs, *ws, ip)


def norm_kernel(parts_ref, right_ref, train_len_ref, roll_len_ref, train_ref, roll_ref):
    left = jnp.sum(parts_ref[...], axis=0)
    token = lax.broadcasted_iota(jnp.int32, (8, RANK), 0)
    for s, (len_ref, ref) in enumerate(((train_len_ref, train_ref), (roll_len_ref, roll_ref))):
        one = jnp.where(token < len_ref[0], left[:, s * RANK : (s + 1) * RANK], 0.0)
        right = right_ref[s]
        grad = lax.dot_general(
            one, right, (((0,), (0,)), ((), ())), precision=HIGH, preferred_element_type=jnp.float32
        )
        mean = jnp.sum(grad * grad) / (RANK * RANK)
        inv = 1.0 / jnp.sqrt(jnp.full((8, RANK), mean + 1e-6))
        ref[...] = jnp.broadcast_to(jnp.concatenate([one * inv, right], axis=-1), ref.shape)


def score_kernel(train_ref, roll_ref, y_ref, out_ref):
    t = train_ref[...].reshape(-1, 2 * RANK)
    r = roll_ref[...].reshape(-1, 2 * RANK)
    dims = (((1,), (1,)), ((), ()))
    a = lax.dot_general(
        r[:, :RANK], t[:, :RANK], dims, precision=HIGH, preferred_element_type=jnp.float32
    )
    b = lax.dot_general(
        r[:, RANK:], t[:, RANK:], dims, precision=HIGH, preferred_element_type=jnp.float32
    )
    both = jnp.sum((a * b).reshape(16, 8, 256), axis=1)
    group = lax.broadcasted_iota(jnp.int32, (256, 32), 0) // 8
    step = group & 3
    step = step ^ (step >> 1)
    column = (group & 28) + ((y_ref[0] - step) & 3)
    pick = (column == lax.broadcasted_iota(jnp.int32, (256, 32), 1)).astype(jnp.float32)
    out_ref[...] = jnp.dot(both, pick, precision=HIGH, preferred_element_type=jnp.float32) / RANK


def shift(n, k):
    return [(i, (i + k) % n) for i in range(n)]


def on_device(
    train_hidden,
    train_cotangent,
    train_lengths,
    roll_hidden,
    roll_cotangent,
    roll_lengths,
    gate_weight,
    up_weight,
    in_project,
    out_project,
):
    x, zh, co, zl, y = (lax.axis_index(a) for a in ("x", "zh", "co", "zl", "y"))
    width = train_hidden.shape[2]
    own = jnp.concatenate([train_hidden[0], roll_hidden[0]], axis=0)
    w = jnp.concatenate([gate_weight, up_weight], axis=1)

    other = lax.ppermute(w, "zh", shift(2, 1))

    block, zls = own, [zl]
    for k in (4, 2):
        got = lax.ppermute(block, "zl", [(i, i ^ k) for i in range(NZL)])
        block, zls = jnp.concatenate([block, got], axis=0), zls + [z ^ k for z in zls]
    twin = lax.ppermute(block, "zl", [(i, i ^ 1) for i in range(NZL)])

    first, second = [1, 0, 3, 2], [3, 2, 1, 0]
    step1 = [(c * NY + i, c * NY + (first, second)[c][i]) for c in range(2) for i in range(NY)]
    step2 = [(c * NY + i, c * NY + (second, first)[c][i]) for c in range(2) for i in range(NY)]
    y1 = jnp.where(co == 0, y ^ 1, 3 - y)
    y2 = jnp.where(co == 0, 3 - y, y ^ 1)
    y3 = y ^ 2
    xs, slots = [], []
    for part, at in ((block, zls), (twin, [z ^ 1 for z in zls])):
        got = lax.ppermute(part, ("co", "y"), step1)
        both = jnp.concatenate([part, got], axis=0)
        xs += [both, lax.ppermute(both, ("co", "y"), step2)]
        slots += [z * NY + o for o in (y, y1, y2, y3) for z in at]

    def over_x(a):
        spread = jnp.broadcast_to(a, (NX,) + a.shape)
        return lax.all_to_all(spread, "x", 0, 0, tiled=True)

    ws, cols = [], []
    for a, h in ((w, zh), (other, 1 - zh)):
        a = over_x(a)
        ws += [a, lax.ppermute(a, "co", shift(2, 1))]
        cols += [(i * 4 + h * 2 + c) * 256 for c in (co, 1 - co) for i in range(NX)]

    parts = mlp(
        jnp.stack(cols).astype(jnp.int32), jnp.stack(slots).astype(jnp.int32), xs, ws, in_project.T
    )
    cot = jnp.concatenate([train_cotangent[0], roll_cotangent[0]], axis=0)
    right = jnp.dot(cot, out_project, preferred_element_type=jnp.float32).reshape(2, 8, RANK)
    parts = lax.all_to_all(parts, ("zl", "y"), 0, 0, tiled=True)
    small = jax.ShapeDtypeStruct((8, 2 * RANK), jnp.float32)
    vmem, smem = pl.BlockSpec(memory_space=pltpu.VMEM), pl.BlockSpec(memory_space=pltpu.SMEM)
    train, roll = pl.pallas_call(
        norm_kernel,
        out_shape=[small, jax.ShapeDtypeStruct((16, 8, 2 * RANK), jnp.float32)],
        in_specs=[vmem, vmem, smem, smem],
        name="norm",
    )(parts, right, train_lengths, roll_lengths)
    roll_all = lax.all_to_all(
        roll, ("x", "zh", "co"), 0, 0, tiled=True
    )
    near = [train] + [lax.ppermute(train, "y", shift(NY, k)) for k in (1, 3, 2)]
    train_all = lax.all_to_all(
        jnp.broadcast_to(jnp.stack(near), (NZL, NY, 8, 2 * RANK)), "zl", 0, 0, tiled=True
    )
    scores = pl.pallas_call(
        score_kernel,
        out_shape=jax.ShapeDtypeStruct((16, 32), jnp.float32),
        in_specs=[vmem, vmem, smem],
        name="score",
    )(train_all, roll_all, y.astype(jnp.int32).reshape(1))
    return scores.T


def solution(mesh):
    fine = Mesh(mesh.devices.reshape(NX, NZH, NCO, NZL, NY), ("x", "zh", "co", "zl", "y"))
    rows, cols = ("x", "zh", "co"), ("zl", "y")
    placed = (
        P(rows + cols, None, None),
        P(rows + cols, None, None),
        P(rows + cols),
        P(cols + rows, None, None),
        P(cols + rows, None, None),
        P(cols + rows),
        P(rows, cols),
        P(rows, cols),
        P(cols, None),
        P(),
    )
    return jax.shard_map(
        on_device, mesh=fine, in_specs=placed, out_specs=P(rows, cols), check_vma=False
    )
```

```python
import functools

import jax
import jax.numpy as jnp
from jax import lax
from jax.experimental import pallas as pl
from jax.experimental.pallas import tpu as pltpu
from jax.sharding import Mesh, PartitionSpec as P

RANK = 64
NX, NZH, NCO, NZL, NY = 4, 2, 2, 8, 4
HIGH = lax.Precision.HIGHEST


def mlp_kernel(nx, nw, cols_ref, slot_ref, *refs):
    x_refs = refs[:nx]
    w_refs = refs[nx : nx + nw]
    ip_ref, out_ref, xv, wv, acc, xsem, wsem = refs[nx + nw :]
    part_k = xv.shape[1] // 4
    groups = []
    for h in range(4):
        at, copies = 0, []
        for i, x_ref in enumerate(x_refs):
            n = x_ref.shape[0]
            cut = pl.ds(h * part_k, part_k)
            copies.append(
                pltpu.make_async_copy(x_ref.at[:, cut], xv.at[pl.ds(at, n), cut], xsem.at[h * nx + i])
            )
            at += n
        for p in range(nw):
            row = pl.multiple_of(cols_ref[p * 4 + h], 256)
            copies.append(
                pltpu.make_async_copy(w_refs[p].at[h], wv.at[pl.ds(row, 256)], wsem.at[p * 4 + h])
            )
        groups.append(copies)
    for copies in groups:
        for c in copies:
            c.start()
    for h, copies in enumerate(groups):
        for c in copies:
            c.wait()
        k = slice(h * part_k, (h + 1) * part_k)
        part = jnp.dot(xv[:, k], wv[k], preferred_element_type=jnp.float32)
        if h:
            acc[...] += part
        else:
            acc[...] = part
    half = acc.shape[1] // 2
    for m in range(4):
        both = acc[m * 128 : (m + 1) * 128]
        gate, up = both[:, :half], both[:, half:]
        act = (gate / (1.0 + jnp.exp(-gate)) * up).astype(jnp.bfloat16)
        left = lax.dot_general(
            act, ip_ref[...], (((1,), (1,)), ((), ())), preferred_element_type=jnp.float32
        )
        left = left.reshape(8, 2, 8, RANK)
        left = jnp.concatenate([left[:, 0], left[:, 1]], axis=-1)
        for i in range(8):
            out_ref[slot_ref[m * 8 + i]] = left[i]


def mlp(cols, slots, xs, ws, ip):
    any_ = pl.BlockSpec(memory_space=pl.ANY)
    smem = pl.BlockSpec(memory_space=pltpu.SMEM)
    nx, nw = len(xs), len(ws)
    return pl.pallas_call(
        functools.partial(mlp_kernel, nx, nw),
        out_shape=jax.ShapeDtypeStruct((32, 8, 2 * RANK), jnp.float32),
        in_specs=[smem, smem] + [any_] * (nx + nw) + [pl.BlockSpec(memory_space=pltpu.VMEM)],
        out_specs=pl.BlockSpec(memory_space=pltpu.VMEM),
        scratch_shapes=[
            pltpu.VMEM((512, xs[0].shape[1]), jnp.bfloat16),
            pltpu.VMEM((4096, ws[0].shape[2]), jnp.bfloat16),
            pltpu.VMEM((512, ws[0].shape[2]), jnp.float32),
            pltpu.SemaphoreType.DMA((4 * nx,)),
            pltpu.SemaphoreType.DMA((4 * nw,)),
        ],
        compiler_params=pltpu.CompilerParams(vmem_limit_bytes=60 << 20),
        name="mlp",
    )(cols, slots, *xs, *ws, ip)


def norm_kernel(parts_ref, right_ref, train_len_ref, roll_len_ref, train_ref, roll_ref):
    left = jnp.sum(parts_ref[...], axis=0)
    token = lax.broadcasted_iota(jnp.int32, (8, RANK), 0)
    for s, (len_ref, ref) in enumerate(((train_len_ref, train_ref), (roll_len_ref, roll_ref))):
        one = jnp.where(token < len_ref[0], left[:, s * RANK : (s + 1) * RANK], 0.0)
        right = right_ref[s]
        grad = lax.dot_general(
            one, right, (((0,), (0,)), ((), ())), precision=HIGH, preferred_element_type=jnp.float32
        )
        mean = jnp.sum(grad * grad) / (RANK * RANK)
        inv = 1.0 / jnp.sqrt(jnp.full((8, RANK), mean + 1e-6))
        both = jnp.concatenate([one * inv, right], axis=-1).astype(ref.dtype)
        ref[...] = jnp.broadcast_to(both, ref.shape)


def score_kernel(train_ref, roll_ref, y_ref, out_ref):
    t = train_ref[...].astype(jnp.float32).reshape(-1, 2 * RANK)
    r = roll_ref[...].reshape(-1, 2 * RANK)
    dims = (((1,), (1,)), ((), ()))
    a = lax.dot_general(
        r[:, :RANK], t[:, :RANK], dims, precision=HIGH, preferred_element_type=jnp.float32
    )
    b = lax.dot_general(
        r[:, RANK:], t[:, RANK:], dims, precision=HIGH, preferred_element_type=jnp.float32
    )
    both = jnp.sum((a * b).reshape(16, 8, 256), axis=1)
    group = lax.broadcasted_iota(jnp.int32, (256, 32), 0) // 8
    step = group & 3
    step = step ^ (step >> 1)
    column = (group & 28) + ((y_ref[0] - step) & 3)
    pick = (column == lax.broadcasted_iota(jnp.int32, (256, 32), 1)).astype(jnp.float32)
    out_ref[...] = jnp.dot(both, pick, precision=HIGH, preferred_element_type=jnp.float32) / RANK


def shift(n, k):
    return [(i, (i + k) % n) for i in range(n)]


def on_device(
    train_hidden,
    train_cotangent,
    train_lengths,
    roll_hidden,
    roll_cotangent,
    roll_lengths,
    gate_weight,
    up_weight,
    in_project,
    out_project,
):
    x, zh, co, zl, y = (lax.axis_index(a) for a in ("x", "zh", "co", "zl", "y"))
    width = train_hidden.shape[2]
    own = jnp.concatenate([train_hidden[0], roll_hidden[0]], axis=0)
    w = jnp.concatenate([gate_weight, up_weight], axis=1)

    other = lax.ppermute(w, "zh", shift(2, 1))

    block, zls = own, [zl]
    for k in (4, 2):
        got = lax.ppermute(block, "zl", [(i, i ^ k) for i in range(NZL)])
        block, zls = jnp.concatenate([block, got], axis=0), zls + [z ^ k for z in zls]
    twin = lax.ppermute(block, "zl", [(i, i ^ 1) for i in range(NZL)])

    first, second = [1, 0, 3, 2], [3, 2, 1, 0]
    step1 = [(c * NY + i, c * NY + (first, second)[c][i]) for c in range(2) for i in range(NY)]
    step2 = [(c * NY + i, c * NY + (second, first)[c][i]) for c in range(2) for i in range(NY)]
    y1 = jnp.where(co == 0, y ^ 1, 3 - y)
    y2 = jnp.where(co == 0, 3 - y, y ^ 1)
    y3 = y ^ 2
    xs, slots = [], []
    for part, at in ((block, zls), (twin, [z ^ 1 for z in zls])):
        got = lax.ppermute(part, ("co", "y"), step1)
        both = jnp.concatenate([part, got], axis=0)
        xs += [both, lax.ppermute(both, ("co", "y"), step2)]
        slots += [z * NY + o for o in (y, y1, y2, y3) for z in at]

    def over_x(a):
        spread = jnp.broadcast_to(a, (NX,) + a.shape)
        return lax.all_to_all(spread, "x", 0, 0, tiled=True)

    ws, cols = [], []
    for a, h in ((w, zh), (other, 1 - zh)):
        a = over_x(a)
        ws += [a, lax.ppermute(a, "co", shift(2, 1))]
        cols += [(i * 4 + h * 2 + c) * 256 for c in (co, 1 - co) for i in range(NX)]

    parts = mlp(
        jnp.stack(cols).astype(jnp.int32), jnp.stack(slots).astype(jnp.int32), xs, ws, in_project.T
    )
    cot = jnp.concatenate([train_cotangent[0], roll_cotangent[0]], axis=0)
    right = jnp.dot(cot, out_project, preferred_element_type=jnp.float32).reshape(2, 8, RANK)
    parts = lax.all_to_all(parts, ("zl", "y"), 0, 0, tiled=True)
    small = jax.ShapeDtypeStruct((8, 2 * RANK), jnp.bfloat16)
    vmem, smem = pl.BlockSpec(memory_space=pltpu.VMEM), pl.BlockSpec(memory_space=pltpu.SMEM)
    train, roll = pl.pallas_call(
        norm_kernel,
        out_shape=[small, jax.ShapeDtypeStruct((16, 8, 2 * RANK), jnp.float32)],
        in_specs=[vmem, vmem, smem, smem],
        name="norm",
    )(parts, right, train_lengths, roll_lengths)
    roll_all = lax.all_to_all(
        roll, ("x", "zh", "co"), 0, 0, tiled=True
    )
    near = [train] + [lax.ppermute(train, "y", shift(NY, k)) for k in (1, 3, 2)]
    train_all = lax.all_to_all(
        jnp.broadcast_to(jnp.stack(near), (NZL, NY, 8, 2 * RANK)), "zl", 0, 0, tiled=True
    )
    scores = pl.pallas_call(
        score_kernel,
        out_shape=jax.ShapeDtypeStruct((16, 32), jnp.float32),
        in_specs=[vmem, vmem, smem],
        name="score",
    )(train_all, roll_all, y.astype(jnp.int32).reshape(1))
    return scores.T


def solution(mesh):
    fine = Mesh(mesh.devices.reshape(NX, NZH, NCO, NZL, NY), ("x", "zh", "co", "zl", "y"))
    rows, cols = ("x", "zh", "co"), ("zl", "y")
    placed = (
        P(rows + cols, None, None),
        P(rows + cols, None, None),
        P(rows + cols),
        P(cols + rows, None, None),
        P(cols + rows, None, None),
        P(cols + rows),
        P(rows, cols),
        P(rows, cols),
        P(cols, None),
        P(),
    )
    return jax.shard_map(
        on_device, mesh=fine, in_specs=placed, out_specs=P(rows, cols), check_vma=False
    )
```

```python
import functools

import jax
import jax.numpy as jnp
from jax import lax
from jax.experimental import pallas as pl
from jax.experimental.pallas import tpu as pltpu
from jax.sharding import Mesh, PartitionSpec as P

RANK = 64
NX, NZH, NCO, NZL, NY = 4, 2, 2, 8, 4
HIGH = lax.Precision.HIGHEST


def mlp_kernel(nx, nw, cols_ref, slot_ref, *refs):
    x_refs = refs[:nx]
    w_refs = refs[nx : nx + nw]
    ip_ref, out_ref, xv, wv, acc, xsem, wsem = refs[nx + nw :]
    part_k = xv.shape[1] // 4
    groups = []
    for h in range(4):
        at, copies = 0, []
        for i, x_ref in enumerate(x_refs):
            n = x_ref.shape[0]
            cut = pl.ds(h * part_k, part_k)
            copies.append(
                pltpu.make_async_copy(x_ref.at[:, cut], xv.at[pl.ds(at, n), cut], xsem.at[h * nx + i])
            )
            at += n
        for p in range(nw):
            row = pl.multiple_of(cols_ref[p * 4 + h], 256)
            copies.append(
                pltpu.make_async_copy(w_refs[p].at[h], wv.at[pl.ds(row, 256)], wsem.at[p * 4 + h])
            )
        groups.append(copies)
    for copies in groups:
        for c in copies:
            c.start()
    for h, copies in enumerate(groups):
        for c in copies:
            c.wait()
        k = slice(h * part_k, (h + 1) * part_k)
        part = jnp.dot(xv[:, k], wv[k], preferred_element_type=jnp.float32)
        if h:
            acc[...] += part
        else:
            acc[...] = part
    half = acc.shape[1] // 2
    for m in range(4):
        both = acc[m * 128 : (m + 1) * 128]
        gate, up = both[:, :half], both[:, half:]
        act = (gate / (1.0 + jnp.exp(-gate)) * up).astype(jnp.bfloat16)
        left = lax.dot_general(
            act, ip_ref[...], (((1,), (1,)), ((), ())), preferred_element_type=jnp.float32
        )
        left = left.reshape(8, 2, 8, RANK)
        left = jnp.concatenate([left[:, 0], left[:, 1]], axis=-1)
        for i in range(8):
            out_ref[slot_ref[m * 8 + i]] = left[i]


def mlp(cols, slots, xs, ws, ip):
    any_ = pl.BlockSpec(memory_space=pl.ANY)
    smem = pl.BlockSpec(memory_space=pltpu.SMEM)
    nx, nw = len(xs), len(ws)
    return pl.pallas_call(
        functools.partial(mlp_kernel, nx, nw),
        out_shape=jax.ShapeDtypeStruct((32, 8, 2 * RANK), jnp.float32),
        in_specs=[smem, smem] + [any_] * (nx + nw) + [pl.BlockSpec(memory_space=pltpu.VMEM)],
        out_specs=pl.BlockSpec(memory_space=pltpu.VMEM),
        scratch_shapes=[
            pltpu.VMEM((512, xs[0].shape[1]), jnp.bfloat16),
            pltpu.VMEM((4096, ws[0].shape[2]), jnp.bfloat16),
            pltpu.VMEM((512, ws[0].shape[2]), jnp.float32),
            pltpu.SemaphoreType.DMA((4 * nx,)),
            pltpu.SemaphoreType.DMA((4 * nw,)),
        ],
        compiler_params=pltpu.CompilerParams(vmem_limit_bytes=60 << 20),
        name="mlp",
    )(cols, slots, *xs, *ws, ip)


def norm_kernel(parts_ref, right_ref, train_len_ref, roll_len_ref, train_ref, roll_ref):
    left = jnp.sum(parts_ref[...], axis=0)
    token = lax.broadcasted_iota(jnp.int32, (8, RANK), 0)
    for s, (len_ref, ref) in enumerate(((train_len_ref, train_ref), (roll_len_ref, roll_ref))):
        one = jnp.where(token < len_ref[0], left[:, s * RANK : (s + 1) * RANK], 0.0)
        right = right_ref[s]
        grad = lax.dot_general(
            one, right, (((0,), (0,)), ((), ())), precision=HIGH, preferred_element_type=jnp.float32
        )
        mean = jnp.sum(grad * grad) / (RANK * RANK)
        inv = 1.0 / jnp.sqrt(jnp.full((8, RANK), mean + 1e-6))
        ref[...] = jnp.broadcast_to(jnp.concatenate([one * inv, right], axis=-1), ref.shape)


def repeat_kernel(*refs):
    for k in range(NY):
        refs[NY][:, k] = jnp.broadcast_to(refs[k][...], (NZL,) + refs[k].shape)


def score_kernel(train_ref, roll_ref, y_ref, out_ref):
    t = train_ref[...].reshape(-1, 2 * RANK)
    r = roll_ref[...].reshape(-1, 2 * RANK)
    dims = (((1,), (1,)), ((), ()))
    a = lax.dot_general(
        r[:, :RANK], t[:, :RANK], dims, precision=HIGH, preferred_element_type=jnp.float32
    )
    b = lax.dot_general(
        r[:, RANK:], t[:, RANK:], dims, precision=HIGH, preferred_element_type=jnp.float32
    )
    both = jnp.sum((a * b).reshape(16, 8, 256), axis=1)
    group = lax.broadcasted_iota(jnp.int32, (256, 32), 0) // 8
    step = group & 3
    step = step ^ (step >> 1)
    column = (group & 28) + ((y_ref[0] - step) & 3)
    pick = (column == lax.broadcasted_iota(jnp.int32, (256, 32), 1)).astype(jnp.float32)
    out_ref[...] = jnp.dot(both, pick, precision=HIGH, preferred_element_type=jnp.float32) / RANK


def shift(n, k):
    return [(i, (i + k) % n) for i in range(n)]


def on_device(
    train_hidden,
    train_cotangent,
    train_lengths,
    roll_hidden,
    roll_cotangent,
    roll_lengths,
    gate_weight,
    up_weight,
    in_project,
    out_project,
):
    x, zh, co, zl, y = (lax.axis_index(a) for a in ("x", "zh", "co", "zl", "y"))
    width = train_hidden.shape[2]
    own = jnp.concatenate([train_hidden[0], roll_hidden[0]], axis=0)
    w = jnp.concatenate([gate_weight, up_weight], axis=1)

    other = lax.ppermute(w, "zh", shift(2, 1))

    block, zls = own, [zl]
    for k in (4, 2):
        got = lax.ppermute(block, "zl", [(i, i ^ k) for i in range(NZL)])
        block, zls = jnp.concatenate([block, got], axis=0), zls + [z ^ k for z in zls]
    twin = lax.ppermute(block, "zl", [(i, i ^ 1) for i in range(NZL)])

    first, second = [1, 0, 3, 2], [3, 2, 1, 0]
    step1 = [(c * NY + i, c * NY + (first, second)[c][i]) for c in range(2) for i in range(NY)]
    step2 = [(c * NY + i, c * NY + (second, first)[c][i]) for c in range(2) for i in range(NY)]
    y1 = jnp.where(co == 0, y ^ 1, 3 - y)
    y2 = jnp.where(co == 0, 3 - y, y ^ 1)
    y3 = y ^ 2
    xs, slots = [], []
    for part, at in ((block, zls), (twin, [z ^ 1 for z in zls])):
        got = lax.ppermute(part, ("co", "y"), step1)
        both = jnp.concatenate([part, got], axis=0)
        xs += [both, lax.ppermute(both, ("co", "y"), step2)]
        slots += [z * NY + o for o in (y, y1, y2, y3) for z in at]

    def over_x(a):
        spread = jnp.broadcast_to(a, (NX,) + a.shape)
        return lax.all_to_all(spread, "x", 0, 0, tiled=True)

    ws, cols = [], []
    for a, h in ((w, zh), (other, 1 - zh)):
        a = over_x(a)
        ws += [a, lax.ppermute(a, "co", shift(2, 1))]
        cols += [(i * 4 + h * 2 + c) * 256 for c in (co, 1 - co) for i in range(NX)]

    parts = mlp(
        jnp.stack(cols).astype(jnp.int32), jnp.stack(slots).astype(jnp.int32), xs, ws, in_project.T
    )
    cot = jnp.concatenate([train_cotangent[0], roll_cotangent[0]], axis=0)
    right = jnp.dot(cot, out_project, preferred_element_type=jnp.float32).reshape(2, 8, RANK)
    parts = lax.all_to_all(parts, ("zl", "y"), 0, 0, tiled=True)
    small = jax.ShapeDtypeStruct((8, 2 * RANK), jnp.float32)
    vmem, smem = pl.BlockSpec(memory_space=pltpu.VMEM), pl.BlockSpec(memory_space=pltpu.SMEM)
    train, roll = pl.pallas_call(
        norm_kernel,
        out_shape=[small, jax.ShapeDtypeStruct((16, 8, 2 * RANK), jnp.float32)],
        in_specs=[vmem, vmem, smem, smem],
        name="norm",
    )(parts, right, train_lengths, roll_lengths)
    roll_all = lax.all_to_all(
        roll, ("x", "zh", "co"), 0, 0, tiled=True
    )
    near = [train] + [lax.ppermute(train, "y", shift(NY, k)) for k in (1, 3, 2)]
    train_all = lax.all_to_all(
        pl.pallas_call(
            repeat_kernel,
            out_shape=jax.ShapeDtypeStruct((NZL, NY, 8, 2 * RANK), jnp.float32),
            name="repeat",
        )(*near),
        "zl",
        0,
        0,
        tiled=True,
    )
    scores = pl.pallas_call(
        score_kernel,
        out_shape=jax.ShapeDtypeStruct((16, 32), jnp.float32),
        in_specs=[vmem, vmem, smem],
        name="score",
    )(train_all, roll_all, y.astype(jnp.int32).reshape(1))
    return scores.T


def solution(mesh):
    fine = Mesh(mesh.devices.reshape(NX, NZH, NCO, NZL, NY), ("x", "zh", "co", "zl", "y"))
    rows, cols = ("x", "zh", "co"), ("zl", "y")
    placed = (
        P(rows + cols, None, None),
        P(rows + cols, None, None),
        P(rows + cols),
        P(cols + rows, None, None),
        P(cols + rows, None, None),
        P(cols + rows),
        P(rows, cols),
        P(rows, cols),
        P(cols, None),
        P(),
    )
    return jax.shard_map(
        on_device, mesh=fine, in_specs=placed, out_specs=P(rows, cols), check_vma=False
    )
```
